128 devices in a mesh: group: 8 (over z, core), rank: 16 (over x, y).
Axes of the slice: x: 4, y: 4, z: 4, core: 2. Of those that a mesh axis runs over, the one named last changes fastest.
Arguments:
- grad_out: bfloat16 [65536, 768], P(('group', 'rank')), may hold values from -6 to 6
- gate_prob: float32 [65536], P(('group', 'rank')), may hold values from 0.2 to 1
- expert_index: int32 [65536], P(('group', 'rank')), may hold values from 0 to 127
- slot: int32 [65536], P(('group', 'rank')), may hold values from -1 to 7, as said below
- saved_inputs: bfloat16 [128, 1024, 768], P(('group', 'rank')), may hold values from -6 to 6
- w_in: bfloat16 [128, 768, 2048], P(('group', 'rank')), may hold values from -0.21875 to 0.21875
- w_out: bfloat16 [128, 2048, 768], P(('group', 'rank')), may hold values from -0.125 to 0.125
Outputs:
- grad_in: bfloat16 [65536, 768], P(('group', 'rank'))
- grad_w_in: float32 [128, 768, 2048], P(('group', 'rank'))
- grad_w_out: float32 [128, 2048, 768], P(('group', 'rank'))
The draws below stay inside these ranges and needn't reach their ends.
Inputs may be any that keep to these rules, and one draw needn't show every extreme that they name: slot[t] is the number of earlier tokens of the same device with the same expert, or -1 where that number is 8 or more.
All inputs are finite; a program needn't handle non-finite values.
Results may differ from the reference program's by a relative error of at most 0.018.
Values may be sent and summed in bfloat16 or wider, within the bound.
A program may use at most 128 MiB of HBM per device.

```python
import jax
import jax.numpy as jnp
from jax import lax

D = 768
FF = 2048
TOK_DEV = 512
EXPERTS = 128
CAP = 8
TOKENS = 65536


def routing(key):
    base = jax.random.fold_in(key, 11)
    keys = jax.random.split(base, 5)
    blocks = TOKENS // TOK_DEV
    first = jax.random.randint(keys[0], (blocks, TOK_DEV), 0, EXPERTS)
    second = jax.random.randint(keys[1], (blocks, TOK_DEV), 0, EXPERTS)
    chosen = jnp.minimum(first, second)
    hot_expert = jax.random.randint(keys[2], (), 0, EXPERTS)
    forced = jax.random.randint(keys[3], (blocks, 1), CAP + 1, 2 * CAP + 1)
    block_keys = jax.random.split(keys[4], blocks)
    ranked = jax.vmap(lambda k: jax.random.permutation(k, TOK_DEV))(block_keys)
    chosen = jnp.where(ranked < forced, hot_expert, chosen)
    chosen = jnp.where(ranked == TOK_DEV - 1, EXPERTS - 1, chosen)
    chosen = jnp.where(ranked == TOK_DEV - 2, 0, chosen)
    same = chosen[:, :, None] == chosen[:, None, :]
    later = jnp.arange(TOK_DEV)[:, None] > jnp.arange(TOK_DEV)[None, :]
    before = jnp.sum((same & later[None, :, :]).astype(jnp.int32), axis=2)
    slots = jnp.where(before < CAP, before, -1)
    return (chosen.reshape(TOKENS).astype(jnp.int32), slots.reshape(TOKENS).astype(jnp.int32))


def draw_expert_index(key, part):
    chosen, slots = routing(key)
    return chosen


def draw_slot(key, part):
    chosen, slots = routing(key)
    return slots


def block_scale(key, extent, shards, smallest, high):
    def one(dim, blocks):
        heights = jax.random.uniform(jax.random.fold_in(jax.random.fold_in(key, 6), dim), (blocks,), jnp.float32, smallest / len(shards), high / len(shards))
        return jnp.repeat(jnp.exp(heights), extent[dim] // blocks).reshape((-1,) + (1,) * (len(extent) - dim - 1))

    factor_of = one(*shards[0])
    for cut in shards[1:]:
        factor_of = factor_of * one(*cut)
    return factor_of


def bell_draw(own_key, dims, spread, reach, shards=(), kind=jnp.bfloat16):
    array = jax.random.normal(own_key, dims, jnp.float32) * spread
    if len(shards) > 0:
        array = block_scale(own_key, dims, shards, -0.22, 0.18) * array
    return jnp.clip(array, min=-reach, max=reach).astype(kind)


def setup_inputs(seed: int = 0) -> dict:
    splits = jax.random.split(jax.random.key(seed), 8)
    return {
        "grad_out": bell_draw(splits[0], (TOKENS, D), 1.0, 6.0, ((0, 128),)),
        "gate_prob": jnp.clip(0.2 + 0.8 * jax.random.uniform(splits[1], (TOKENS,), jnp.float32) ** block_scale(splits[1], (TOKENS,), ((0, 128),), -0.2, 0.2), 0.2, 1.0),
        "expert_index": draw_expert_index(jax.random.fold_in(splits[7], 71), 0),
        "slot": draw_slot(jax.random.fold_in(splits[7], 71), 0),
        "saved_inputs": bell_draw(splits[4], (EXPERTS, EXPERTS * CAP, D), 1.0, 6.0, ((0, 128),)),
        "w_in": bell_draw(splits[5], (EXPERTS, D, FF), D ** -0.5, 0.21875, ((0, 128),)),
        "w_out": bell_draw(splits[6], (EXPERTS, FF, D), FF ** -0.5, 0.125, ((0, 128),)),
    }


def reference(grad_out, gate_prob, expert_index, slot, saved_inputs, w_in, w_out):
    scaled = (gate_prob[:, None] * grad_out.astype(jnp.float32)).astype(jnp.bfloat16)
    positions = jnp.arange(TOKENS, dtype=jnp.int32)
    source = positions // TOK_DEV
    kept = slot >= 0
    rows_total = EXPERTS * EXPERTS * CAP
    row = jnp.where(kept, expert_index * (EXPERTS * CAP) + source * CAP + slot, rows_total).astype(jnp.int32)
    owner = jnp.zeros((rows_total + 1,), jnp.int32).at[row].set(positions + 1)
    owner = owner[:rows_total].reshape(EXPERTS, EXPERTS * CAP)

    def one_expert(items):
        inputs, first, second, owned = items
        picked = jnp.take(scaled, jnp.maximum(owned - 1, 0), axis=0)
        grad_rows = jnp.where(owned[:, None] > 0, picked, jnp.zeros_like(picked))
        pre = jnp.dot(inputs, first, preferred_element_type=jnp.float32)
        hidden = jnp.maximum(pre, 0.0).astype(jnp.bfloat16)
        grad_second = jnp.dot(hidden.T, grad_rows, preferred_element_type=jnp.float32)
        back = jnp.dot(grad_rows, second.T, preferred_element_type=jnp.float32)
        grad_hidden = jnp.where(pre > 0, back, jnp.zeros_like(back)).astype(jnp.bfloat16)
        grad_first = jnp.dot(inputs.T, grad_hidden, preferred_element_type=jnp.float32)
        row_grad = jnp.dot(grad_hidden, first.T, preferred_element_type=jnp.float32).astype(jnp.bfloat16)
        return grad_first, grad_second, row_grad

    grad_w_in, grad_w_out, row_grad = lax.map(one_expert, (saved_inputs, w_in, w_out, owner))
    flat = row_grad.reshape(rows_total, D)
    taken = jnp.take(flat, jnp.minimum(row, rows_total - 1), axis=0)
    grad_in = jnp.where(kept[:, None], taken, jnp.zeros_like(taken))
    return grad_in, grad_w_in, grad_w_out
```

```python
import functools

import jax
import jax.numpy as jnp
from jax import lax
from jax.experimental import pallas as pl
from jax.experimental.pallas import tpu as pltpu
from jax.sharding import PartitionSpec as P

MESH = pl.DeviceIdType.MESH
BF16, F32 = jnp.bfloat16, jnp.float32
NT = (((1,), (1,)), ((), ()))
TN = (((0,), (0,)), ((), ()))
GROUPS = (((1, 0), (3, 0)), ((1, 1), (3, 1)), ((2, 0), (0, 1)), ((2, 1), (0, 0)))
CAP = 8
SIDE = 4


def dot(a, b, dims=(((1,), (0,)), ((), ()))):
    return lax.dot_general(a, b, dims, preferred_element_type=F32)


def exchange_kernel(
    gate_ref, expert_ref, slot_ref, grad_hbm, inputs_hbm, w_in_hbm, w_out_hbm,
    back_ref, pick_ref, grad_first_ref, grad_second_ref,
    grad, inputs, inputs_t, w_in, w_out, sent, arrived, row_grad, hidden, grad_hidden,
    load_sem, own_sem, send_sem, recv_sem, sync_a, sync_b,
):
    group, rank = lax.axis_index("group"), lax.axis_index("rank")
    x, y, z, core = rank // SIDE, rank % SIDE, group // 2, group % 2
    me = group * 16 + rank
    tokens, width = grad.shape
    rows = inputs.shape[0]
    hid = hidden.shape[1]
    quarter = rows // 4

    def device(dx, dy, dz, dc):
        return (lax.rem(z + dz, SIDE) * 2 + lax.rem(core + dc, 2), lax.rem(x + dx, SIDE) * SIDE + lax.rem(y + dy, SIDE))

    barrier = pltpu.get_barrier_semaphore()
    along_x = [device(i, 0, 0, c) for i in range(4) for c in range(2) if i + c > 0]
    along_y = [device(0, i, 0, 0) for i in (1, 2, 3)]
    along_z = [device(0, 0, i, 0) for i in (1, 2, 3)]
    for d in along_x + along_y + along_z:
        pl.semaphore_signal(barrier, inc=1, device_id=d, device_id_type=MESH)

    load_grad = pltpu.make_async_copy(grad_hbm, grad, load_sem.at[0])
    load_grad.start()
    load_w_in = pltpu.make_async_copy(w_in_hbm, w_in, load_sem.at[1])
    load_w_in.start()
    load_rows = []
    for j, pair in enumerate(GROUPS):
        for i, (dz, dc) in enumerate(pair):
            g = lax.rem(z + dz, SIDE) * 2 + lax.rem(core + dc, 2)
            at = (j * 2 + i) * 128
            load_rows.append(
                pltpu.make_async_copy(
                    inputs_hbm.at[pl.ds(pl.multiple_of(g * 128, 128), 128)], inputs.at[pl.ds(at, 128)], load_sem.at[2 + j * 2 + i]
                )
            )
            load_rows[-1].start()
    load_w_out = pltpu.make_async_copy(w_out_hbm, w_out, load_sem.at[10])
    load_w_out.start()

    gate = gate_ref[...]
    high = gate.astype(BF16)
    rest = gate - high.astype(F32)
    middle = rest.astype(BF16)
    low = (rest - middle.astype(F32)).astype(BF16)
    gates = [jnp.broadcast_to(part, (128, tokens)) for part in (high, middle, low)]
    target = jnp.where(slot_ref[...] >= 0, expert_ref[...] * CAP + slot_ref[...], -1)
    load_grad.wait()

    def fill(q):
        at = lax.broadcasted_iota(jnp.int32, (quarter, tokens), 0) + q * quarter
        table = (at == target).astype(BF16)
        pick_ref[pl.ds(pl.multiple_of(q * quarter, quarter), quarter), :] = table
        factor = dot(table, gates[0], NT) + dot(table, gates[1], NT) + dot(table, gates[2], NT)
        factor = jnp.concatenate([factor] * (width // 128), axis=1)
        block = dot(table, grad[...]) * factor
        sent[pl.ds(q * (quarter // CAP), quarter // CAP)] = block.reshape(quarter // CAP, CAP, width).astype(BF16)

    fill(0)
    pl.semaphore_wait(barrier, 13)
    for d in along_y:
        pl.semaphore_signal(sync_a, inc=1, device_id=d, device_id_type=MESH)
    fill(1)
    pl.semaphore_wait(sync_a, 3)
    for d in along_z:
        pl.semaphore_signal(sync_b, inc=1, device_id=d, device_id_type=MESH)
    fill(2)
    fill(3)
    pl.semaphore_wait(sync_b, 3)

    def send(j, out):
        for i, (dz, dc) in enumerate(GROUPS[j]):
            own = dz == 0 and dc == 0
            g = lax.rem(z + dz, SIDE) * 2 + lax.rem(core + dc, 2)
            there = i if dz in (0, 2) else 1 - i

            def one(k, carry):
                r = lax.rem(x + k // SIDE, SIDE) * SIDE + lax.rem(y + k % SIDE, SIDE)
                if out:
                    src, dst = sent.at[g * 16 + r], arrived.at[(j * 2 + there) * 16 + rank]
                    sems = (send_sem.at[0], recv_sem.at[j])
                else:
                    src, dst = row_grad.at[(j * 2 + i) * 16 + r], back_ref.at[me]
                    sems = (send_sem.at[1], recv_sem.at[4])
                pltpu.make_async_remote_copy(src, dst, *sems, device_id=(g, r), device_id_type=MESH).start()
                return carry

            lax.fori_loop(1 if own else 0, 16, one, 0)
            if own:
                if out:
                    pltpu.make_async_copy(sent.at[me], arrived.at[(j * 2 + i) * 16 + rank], own_sem).start()
                else:
                    pltpu.make_async_copy(row_grad.at[(j * 2 + i) * 16 + rank], back_ref.at[me], own_sem).start()

    for j in range(4):
        send(j, True)

    load_w_in.wait()
    for c in load_rows:
        c.wait()

    @pl.loop(0, 4)
    def _(p):
        at = pl.ds(pl.multiple_of(p * quarter, quarter), quarter)
        for n in range(0, hid, 512):
            pre = dot(inputs[at, :], w_in[:, n : n + 512])
            hidden[at, n : n + 512] = jnp.maximum(pre, 0.0).astype(BF16)

    inputs_t[...] = inputs[...].T
    load_w_out.wait()

    for j in range(4):
        count = 31 if (0, 0) in GROUPS[j] else 32
        got = arrived.at[pl.ds(0, count)]
        pltpu.make_async_copy(got, got, recv_sem.at[j]).wait()
        if count == 31:
            pltpu.make_async_copy(sent.at[me], arrived.at[j * 32 + rank], own_sem).wait()
        block = arrived[pl.ds(j * 32, 32)].reshape(quarter, width)
        at = pl.ds(j * quarter, quarter)
        for n in range(0, hid, 512):
            up = dot(block, w_out[n : n + 512, :], NT)
            grad_hidden[at, n : n + 512] = jnp.where(hidden[at, n : n + 512].astype(F32) > 0, up, 0.0).astype(BF16)
        down = dot(grad_hidden[at, :], w_in[...], NT)
        row_grad[pl.ds(j * 32, 32)] = down.reshape(32, CAP, width).astype(BF16)
        send(j, False)

    @pl.loop(0, hid, step=256)
    def _(n):
        at = pl.ds(pl.multiple_of(n, 256), 256)
        grad_second_ref[at, :] = dot(hidden[:, at], arrived[...].reshape(rows, width), TN)

    @pl.loop(0, hid, step=256)
    def _(n):
        at = pl.ds(pl.multiple_of(n, 256), 256)
        grad_first_ref[:, at] = dot(inputs_t[...], grad_hidden[:, at])

    pltpu.make_async_copy(row_grad.at[0], back_ref.at[me], own_sem).wait()
    most = sent.at[pl.ds(0, 127)]
    pltpu.make_async_copy(most, most, send_sem.at[0]).wait()
    most = row_grad.at[pl.ds(0, 127)]
    pltpu.make_async_copy(most, most, send_sem.at[1]).wait()
    most = back_ref.at[pl.ds(0, 127)]
    pltpu.make_async_copy(most, most, recv_sem.at[4]).wait()


def finish_kernel(back_ref, pick_ref, first_ref, second_ref, grad_in_hbm, first_hbm, second_hbm, grad_in, sems):
    copies = [
        pltpu.make_async_copy(first_ref, first_hbm, sems.at[0]),
        pltpu.make_async_copy(second_ref, second_hbm, sems.at[1]),
    ]
    for c in copies:
        c.start()
    rows, tokens = pick_ref.shape
    grad_in[...] = dot(pick_ref[...], back_ref[...].reshape(rows, grad_in.shape[1]), TN).astype(BF16)
    copies.append(pltpu.make_async_copy(grad_in, grad_in_hbm, sems.at[2]))
    copies[-1].start()
    for c in copies:
        c.wait()


def local(grad_out, gate_prob, expert_index, slot, saved_inputs, w_in, w_out):
    tokens, width = grad_out.shape
    rows, hid = saved_inputs.shape[1], w_in.shape[2]
    experts = rows // CAP
    vmem, hbm = pl.BlockSpec(memory_space=pltpu.VMEM), pl.BlockSpec(memory_space=pl.ANY)
    back, pick, first, second = pl.pallas_call(
        exchange_kernel,
        out_shape=(
            pltpu.VMEM((experts, CAP, width), BF16),
            pltpu.VMEM((rows, tokens), BF16),
            pltpu.VMEM((width, hid), F32),
            pltpu.VMEM((hid, width), F32),
        ),
        in_specs=[vmem] * 3 + [hbm] * 4,
        out_specs=(vmem,) * 4,
        scratch_shapes=[
            pltpu.VMEM((tokens, width), BF16),
            pltpu.VMEM((rows, width), BF16),
            pltpu.VMEM((width, rows), BF16),
            pltpu.VMEM((width, hid), BF16),
            pltpu.VMEM((hid, width), BF16),
            pltpu.VMEM((experts, CAP, width), BF16),
            pltpu.VMEM((experts, CAP, width), BF16),
            pltpu.VMEM((experts, CAP, width), BF16),
            pltpu.VMEM((rows, hid), BF16),
            pltpu.VMEM((rows, hid), BF16),
            pltpu.SemaphoreType.DMA((11,)),
            pltpu.SemaphoreType.DMA,
            pltpu.SemaphoreType.DMA((2,)),
            pltpu.SemaphoreType.DMA((5,)),
            pltpu.SemaphoreType.REGULAR,
            pltpu.SemaphoreType.REGULAR,
        ],
        name="exchange",
        compiler_params=pltpu.CompilerParams(collective_id=0, has_side_effects=True, vmem_limit_bytes=40 << 20),
    )(
        gate_prob.reshape(1, tokens),
        expert_index.reshape(1, tokens),
        slot.reshape(1, tokens),
        grad_out,
        saved_inputs[0],
        w_in[0],
        w_out[0],
    )
    grad_in, grad_first, grad_second = pl.pallas_call(
        finish_kernel,
        out_shape=(
            jax.ShapeDtypeStruct((tokens, width), BF16),
            jax.ShapeDtypeStruct((width, hid), F32),
            jax.ShapeDtypeStruct((hid, width), F32),
        ),
        in_specs=[vmem] * 4,
        out_specs=(hbm,) * 3,
        scratch_shapes=[pltpu.VMEM((tokens, width), BF16), pltpu.SemaphoreType.DMA((3,))],
        name="finish",
        compiler_params=pltpu.CompilerParams(vmem_limit_bytes=24 << 20),
    )(*(pltpu.with_memory_space_constraint(a, pltpu.VMEM) for a in (back, pick, first, second)))
    return grad_in, grad_first[None], grad_second[None]


def solution(mesh):
    spec1, spec2, spec3 = (P(("group", "rank"), *(None,) * n) for n in range(3))
    return jax.shard_map(
        local,
        mesh=mesh,
        in_specs=(spec2, spec1, spec1, spec1, spec3, spec3, spec3),
        out_specs=(spec2, spec3, spec3),
        check_vma=False,
    )
```

```python
import functools

import jax
import jax.numpy as jnp
from jax import lax
from jax.experimental import pallas as pl
from jax.experimental.pallas import tpu as pltpu
from jax.sharding import PartitionSpec as P

MESH = pl.DeviceIdType.MESH
BF16, F32 = jnp.bfloat16, jnp.float32
NT = (((1,), (1,)), ((), ()))
TN = (((0,), (0,)), ((), ()))
GROUPS = (((1, 0), (3, 0)), ((1, 1), (3, 1)), ((2, 0), (0, 1)), ((2, 1), (0, 0)))
CAP = 8
SIDE = 4
PIECES = 1


def dot(a, b, dims=(((1,), (0,)), ((), ()))):
    return lax.dot_general(a, b, dims, preferred_element_type=F32)


def exchange_kernel(
    gate_ref, expert_ref, slot_ref, grad_hbm, inputs_hbm, w_in_hbm, w_out_hbm,
    back_ref, pick_ref, grad_first_ref, grad_second_ref,
    grad, inputs, inputs_t, w_in, w_out, sent, arrived, row_grad, hidden, grad_hidden,
    load_sem, own_sem, send_sem, recv_sem, sync_a, sync_b,
):
    group, rank = lax.axis_index("group"), lax.axis_index("rank")
    x, y, z, core = rank // SIDE, rank % SIDE, group // 2, group % 2
    me = group * 16 + rank
    tokens, width = grad.shape
    rows = inputs.shape[0]
    hid = hidden.shape[1]
    quarter = rows // 4

    def device(dx, dy, dz, dc):
        return (lax.rem(z + dz, SIDE) * 2 + lax.rem(core + dc, 2), lax.rem(x + dx, SIDE) * SIDE + lax.rem(y + dy, SIDE))

    barrier = pltpu.get_barrier_semaphore()
    along_x = [device(i, 0, 0, c) for i in range(4) for c in range(2) if i + c > 0]
    along_y = [device(0, i, 0, 0) for i in (1, 2, 3)]
    along_z = [device(0, 0, i, 0) for i in (1, 2, 3)]
    for d in along_x + along_y + along_z:
        pl.semaphore_signal(barrier, inc=1, device_id=d, device_id_type=MESH)

    load_grad = pltpu.make_async_copy(grad_hbm, grad, load_sem.at[0])
    load_grad.start()
    load_w_in = pltpu.make_async_copy(w_in_hbm, w_in, load_sem.at[1])
    load_w_in.start()
    load_rows = []
    for j, pair in enumerate(GROUPS):
        for i, (dz, dc) in enumerate(pair):
            g = lax.rem(z + dz, SIDE) * 2 + lax.rem(core + dc, 2)
            at = (j * 2 + i) * 128
            load_rows.append(
                pltpu.make_async_copy(
                    inputs_hbm.at[pl.ds(pl.multiple_of(g * 128, 128), 128)], inputs.at[pl.ds(at, 128)], load_sem.at[2 + j * 2 + i]
                )
            )
            load_rows[-1].start()
    load_w_out = pltpu.make_async_copy(w_out_hbm, w_out, load_sem.at[10])
    load_w_out.start()

    gate = gate_ref[...]
    high = gate.astype(BF16)
    rest = gate - high.astype(F32)
    middle = rest.astype(BF16)
    low = (rest - middle.astype(F32)).astype(BF16)
    gates = [jnp.broadcast_to(part, (128, tokens)) for part in (high, middle, low)]
    target = jnp.where(slot_ref[...] >= 0, expert_ref[...] * CAP + slot_ref[...], -1)
    pl.semaphore_wait(barrier, 13)
    for d in along_y:
        pl.semaphore_signal(sync_a, inc=1, device_id=d, device_id_type=MESH)
    pl.semaphore_wait(sync_a, 3)
    for d in along_z:
        pl.semaphore_signal(sync_b, inc=1, device_id=d, device_id_type=MESH)
    load_grad.wait()

    def group_at(j, i):
        dz, dc = GROUPS[j][i]
        return lax.rem(z + dz, SIDE) * 2 + lax.rem(core + dc, 2)

    def fill(g):
        at = lax.broadcasted_iota(jnp.int32, (128, tokens), 0) + g * 128
        table = (at == target).astype(BF16)
        pick_ref[pl.ds(pl.multiple_of(g * 128, 128), 128), :] = table
        factor = dot(table, gates[0], NT) + dot(table, gates[1], NT) + dot(table, gates[2], NT)
        factor = jnp.concatenate([factor] * (width // 128), axis=1)
        block = dot(table, grad[...]) * factor
        sent[pl.ds(g * 16, 16)] = block.reshape(16, CAP, width).astype(BF16)

    def send(j, out):
        def copy_of(i, dx, dy):
            g = group_at(j, i)
            there = i if GROUPS[j][i][0] in (0, 2) else 1 - i
            r = lax.rem(x + dx, SIDE) * SIDE + lax.rem(y + dy, SIDE)
            if out:
                src, dst, end = sent.at[g * 16 + r], arrived.at[(j * 2 + there) * 16 + rank], (send_sem.at[0], recv_sem.at[j])
            else:
                src, dst, end = row_grad.at[(j * 2 + i) * 16 + r], back_ref.at[me], (send_sem.at[1], recv_sem.at[4])
            return src, dst, end, (g, r)

        def start(i, dx, dy):
            src, dst, end, d = copy_of(i, dx, dy)
            pltpu.make_async_remote_copy(src, dst, *end, device_id=d, device_id_type=MESH).start()

        def swing(q):
            return q + q // 2 - 2 * (q // 3)

        def one(k, carry):
            for i in range(2):
                start(i, swing(k % 4), swing((k + k // 4) % 4))
            return carry

        own = (0, 0) in GROUPS[j]
        if own:
            start(0, 0, 0)
            src, dst, _, _ = copy_of(1, 0, 0)
            pltpu.make_async_copy(src, dst, own_sem).start()
        lax.fori_loop(1 if own else 0, 16, one, 0)

    for j in range(4):
        fill(group_at(j, 0))
        fill(group_at(j, 1))
        if j == 0:
            pl.semaphore_wait(sync_b, 3)
        send(j, True)

    load_w_in.wait()
    for c in load_rows:
        c.wait()

    @pl.loop(0, 4)
    def _(p):
        at = pl.ds(pl.multiple_of(p * quarter, quarter), quarter)
        for n in range(0, hid, 512):
            pre = dot(inputs[at, :], w_in[:, n : n + 512])
            hidden[at, n : n + 512] = jnp.maximum(pre, 0.0).astype(BF16)

    inputs_t[...] = inputs[...].T
    load_w_out.wait()

    for j in range(4):
        count = 31 if (0, 0) in GROUPS[j] else 32
        got = arrived.at[pl.ds(0, count)]
        pltpu.make_async_copy(got, got, recv_sem.at[j]).wait()
        if count == 31:
            pltpu.make_async_copy(sent.at[me], arrived.at[j * 32 + rank], own_sem).wait()
        block = arrived[pl.ds(j * 32, 32)].reshape(quarter, width)
        at = pl.ds(j * quarter, quarter)
        for n in range(0, hid, 512):
            up = dot(block, w_out[n : n + 512, :], NT)
            grad_hidden[at, n : n + 512] = jnp.where(hidden[at, n : n + 512].astype(F32) > 0, up, 0.0).astype(BF16)
        down = dot(grad_hidden[at, :], w_in[...], NT)
        row_grad[pl.ds(j * 32, 32)] = down.reshape(32, CAP, width).astype(BF16)
        send(j, False)

    @pl.loop(0, hid, step=256)
    def _(n):
        at = pl.ds(pl.multiple_of(n, 256), 256)
        grad_second_ref[at, :] = dot(hidden[:, at], arrived[...].reshape(rows, width), TN)

    @pl.loop(0, hid, step=256)
    def _(n):
        at = pl.ds(pl.multiple_of(n, 256), 256)
        grad_first_ref[:, at] = dot(inputs_t[...], grad_hidden[:, at])

    pltpu.make_async_copy(row_grad.at[0], back_ref.at[me], own_sem).wait()
    most = sent.at[pl.ds(0, 127)]
    pltpu.make_async_copy(most, most, send_sem.at[0]).wait()
    most = row_grad.at[pl.ds(0, 127)]
    pltpu.make_async_copy(most, most, send_sem.at[1]).wait()
    most = back_ref.at[pl.ds(0, 127)]
    pltpu.make_async_copy(most, most, recv_sem.at[4]).wait()


def finish_kernel(back_ref, pick_ref, first_ref, second_ref, grad_in_hbm, first_hbm, second_hbm, grad_in, sems):
    copies = []
    for ref, to, base in ((first_ref, first_hbm, 0), (second_ref, second_hbm, PIECES)):
        step = ref.shape[0] // PIECES
        for p in range(PIECES):
            at = pl.ds(p * step, step)
            copies.append(pltpu.make_async_copy(ref.at[at], to.at[at], sems.at[base + p]))
            copies[-1].start()
    rows, tokens = pick_ref.shape
    grad_in[...] = dot(pick_ref[...], back_ref[...].reshape(rows, grad_in.shape[1]), TN).astype(BF16)
    copies.append(pltpu.make_async_copy(grad_in, grad_in_hbm, sems.at[2 * PIECES]))
    copies[-1].start()
    for c in copies:
        c.wait()


def local(grad_out, gate_prob, expert_index, slot, saved_inputs, w_in, w_out):
    tokens, width = grad_out.shape
    rows, hid = saved_inputs.shape[1], w_in.shape[2]
    experts = rows // CAP
    vmem, hbm = pl.BlockSpec(memory_space=pltpu.VMEM), pl.BlockSpec(memory_space=pl.ANY)
    back, pick, first, second = pl.pallas_call(
        exchange_kernel,
        out_shape=(
            pltpu.VMEM((experts, CAP, width), BF16),
            pltpu.VMEM((rows, tokens), BF16),
            pltpu.VMEM((width, hid), F32),
            pltpu.VMEM((hid, width), F32),
        ),
        in_specs=[vmem] * 3 + [hbm] * 4,
        out_specs=(vmem,) * 4,
        scratch_shapes=[
            pltpu.VMEM((tokens, width), BF16),
            pltpu.VMEM((rows, width), BF16),
            pltpu.VMEM((width, rows), BF16),
            pltpu.VMEM((width, hid), BF16),
            pltpu.VMEM((hid, width), BF16),
            pltpu.VMEM((experts, CAP, width), BF16),
            pltpu.VMEM((experts, CAP, width), BF16),
            pltpu.VMEM((experts, CAP, width), BF16),
            pltpu.VMEM((rows, hid), BF16),
            pltpu.VMEM((rows, hid), BF16),
            pltpu.SemaphoreType.DMA((11,)),
            pltpu.SemaphoreType.DMA,
            pltpu.SemaphoreType.DMA((2,)),
            pltpu.SemaphoreType.DMA((5,)),
            pltpu.SemaphoreType.REGULAR,
            pltpu.SemaphoreType.REGULAR,
        ],
        name="exchange",
        compiler_params=pltpu.CompilerParams(collective_id=0, has_side_effects=True, vmem_limit_bytes=40 << 20),
    )(
        gate_prob.reshape(1, tokens),
        expert_index.reshape(1, tokens),
        slot.reshape(1, tokens),
        grad_out,
        saved_inputs[0],
        w_in[0],
        w_out[0],
    )
    grad_in, grad_first, grad_second = pl.pallas_call(
        finish_kernel,
        out_shape=(
            jax.ShapeDtypeStruct((tokens, width), BF16),
            jax.ShapeDtypeStruct((width, hid), F32),
            jax.ShapeDtypeStruct((hid, width), F32),
        ),
        in_specs=[vmem] * 4,
        out_specs=(hbm,) * 3,
        scratch_shapes=[pltpu.VMEM((tokens, width), BF16), pltpu.SemaphoreType.DMA((2 * PIECES + 1,))],
        name="finish",
        compiler_params=pltpu.CompilerParams(vmem_limit_bytes=24 << 20),
    )(*(pltpu.with_memory_space_constraint(a, pltpu.VMEM) for a in (back, pick, first, second)))
    return grad_in, grad_first[None], grad_second[None]


def solution(mesh):
    spec1, spec2, spec3 = (P(("group", "rank"), *(None,) * n) for n in range(3))
    return jax.shard_map(
        local,
        mesh=mesh,
        in_specs=(spec2, spec1, spec1, spec1, spec3, spec3, spec3),
        out_specs=(spec2, spec3, spec3),
        check_vma=False,
    )
```

```python
import functools

import jax
import jax.numpy as jnp
from jax import lax
from jax.experimental import pallas as pl
from jax.experimental.pallas import tpu as pltpu
from jax.sharding import PartitionSpec as P

MESH = pl.DeviceIdType.MESH
BF16, F32 = jnp.bfloat16, jnp.float32
NT = (((1,), (1,)), ((), ()))
TN = (((0,), (0,)), ((), ()))
GROUPS = (((1, 0), (3, 0)), ((2, 0), (0, 1)), ((1, 1), (3, 1)), ((2, 1), (0, 0)))
CAP = 8
SIDE = 4
PIECES = 1


def dot(a, b, dims=(((1,), (0,)), ((), ()))):
    return lax.dot_general(a, b, dims, preferred_element_type=F32)


def exchange_kernel(
    gate_hbm, expert_hbm, slot_hbm, grad_hbm, inputs_hbm, w_in_hbm, w_out_hbm,
    back_ref, pick_ref, grad_first_ref, grad_second_ref,
    gate_ref, expert_ref, slot_ref, grad, inputs, inputs_t, w_in, w_out, sent, arrived, row_grad, hidden, grad_hidden,
    load_sem, own_sem, send_sem, recv_sem, sync_a, sync_b,
):
    group, rank = lax.axis_index("group"), lax.axis_index("rank")
    x, y, z, core = rank // SIDE, rank % SIDE, group // 2, group % 2
    me = group * 16 + rank
    tokens, width = grad.shape
    rows = inputs.shape[0]
    hid = hidden.shape[1]
    quarter = rows // 4

    def device(dx, dy, dz, dc):
        return (lax.rem(z + dz, SIDE) * 2 + lax.rem(core + dc, 2), lax.rem(x + dx, SIDE) * SIDE + lax.rem(y + dy, SIDE))

    barrier = pltpu.get_barrier_semaphore()
    others = [device(i, k, l, c) for l in (1, 3, 2, 0) for k in range(4) for i in range(4) for c in range(2) if i + k + l + c > 0]
    for d in others:
        pl.semaphore_signal(barrier, inc=1, device_id=d, device_id_type=MESH)

    load_tokens = [
        pltpu.make_async_copy(src, dst, load_sem.at[11 + i])
        for i, (src, dst) in enumerate(((gate_hbm, gate_ref), (expert_hbm, expert_ref), (slot_hbm, slot_ref)))
    ]
    for c in load_tokens:
        c.start()
    load_grad = pltpu.make_async_copy(grad_hbm, grad, load_sem.at[0])
    load_grad.start()
    load_w_in = pltpu.make_async_copy(w_in_hbm, w_in, load_sem.at[1])
    load_w_in.start()
    load_rows = []
    for j, pair in enumerate(GROUPS):
        for i, (dz, dc) in enumerate(pair):
            g = lax.rem(z + dz, SIDE) * 2 + lax.rem(core + dc, 2)
            at = (j * 2 + i) * 128
            load_rows.append(
                pltpu.make_async_copy(
                    inputs_hbm.at[pl.ds(pl.multiple_of(g * 128, 128), 128)], inputs.at[pl.ds(at, 128)], load_sem.at[2 + j * 2 + i]
                )
            )
            load_rows[-1].start()
    load_w_out = pltpu.make_async_copy(w_out_hbm, w_out, load_sem.at[10])
    load_w_out.start()

    for c in load_tokens:
        c.wait()
    gate = gate_ref[...]
    high = gate.astype(BF16)
    rest = gate - high.astype(F32)
    middle = rest.astype(BF16)
    low = (rest - middle.astype(F32)).astype(BF16)
    gates = [jnp.broadcast_to(part, (128, tokens)) for part in (high, middle, low)]
    target = jnp.where(slot_ref[...] >= 0, expert_ref[...] * CAP + slot_ref[...], -1)
    load_grad.wait()

    def group_at(j, i):
        dz, dc = GROUPS[j][i]
        return lax.rem(z + dz, SIDE) * 2 + lax.rem(core + dc, 2)

    def fill(g):
        at = lax.broadcasted_iota(jnp.int32, (128, tokens), 0) + g * 128
        table = (at == target).astype(BF16)
        pick_ref[pl.ds(pl.multiple_of(g * 128, 128), 128), :] = table
        factor = dot(table, gates[0], NT) + dot(table, gates[1], NT) + dot(table, gates[2], NT)
        factor = jnp.concatenate([factor] * (width // 128), axis=1)
        block = dot(table, grad[...]) * factor
        sent[pl.ds(g * 16, 16)] = block.reshape(16, CAP, width).astype(BF16)

    def send(j, out):
        def copy_of(i, dx, dy):
            g = group_at(j, i)
            there = i if GROUPS[j][i][0] in (0, 2) else 1 - i
            r = lax.rem(x + dx, SIDE) * SIDE + lax.rem(y + dy, SIDE)
            if out:
                src, dst, end = sent.at[g * 16 + r], arrived.at[(j * 2 + there) * 16 + rank], (send_sem.at[0], recv_sem.at[j])
            else:
                src, dst, end = row_grad.at[(j * 2 + i) * 16 + r], back_ref.at[me], (send_sem.at[1], recv_sem.at[4])
            return src, dst, end, (g, r)

        def start(i, dx, dy):
            src, dst, end, d = copy_of(i, dx, dy)
            pltpu.make_async_remote_copy(src, dst, *end, device_id=d, device_id_type=MESH).start()

        def swing(q):
            return q + q // 2 - 2 * (q // 3)

        def one(k, carry):
            for i in range(2):
                start(i, swing(k % 4), swing((k + k // 4) % 4))
            return carry

        own = (0, 0) in GROUPS[j]
        if own:
            start(0, 0, 0)
            src, dst, _, _ = copy_of(1, 0, 0)
            pltpu.make_async_copy(src, dst, own_sem).start()
        lax.fori_loop(1 if own else 0, 16, one, 0)

    for j in range(4):
        fill(group_at(j, 0))
        fill(group_at(j, 1))
        if j == 0:
            pl.semaphore_wait(barrier, 127)
        send(j, True)

    load_w_in.wait()
    for c in load_rows:
        c.wait()

    @pl.loop(0, 4)
    def _(p):
        at = pl.ds(pl.multiple_of(p * quarter, quarter), quarter)
        for n in range(0, hid, 512):
            pre = dot(inputs[at, :], w_in[:, n : n + 512])
            hidden[at, n : n + 512] = jnp.maximum(pre, 0.0).astype(BF16)

    inputs_t[...] = inputs[...].T
    load_w_out.wait()

    for j in range(4):
        count = 31 if (0, 0) in GROUPS[j] else 32
        got = arrived.at[pl.ds(0, count)]
        pltpu.make_async_copy(got, got, recv_sem.at[j]).wait()
        if count == 31:
            pltpu.make_async_copy(sent.at[me], arrived.at[j * 32 + rank], own_sem).wait()
        block = arrived[pl.ds(j * 32, 32)].reshape(quarter, width)
        at = pl.ds(j * quarter, quarter)
        for n in range(0, hid, 512):
            up = dot(block, w_out[n : n + 512, :], NT)
            grad_hidden[at, n : n + 512] = jnp.where(hidden[at, n : n + 512].astype(F32) > 0, up, 0.0).astype(BF16)
        down = dot(grad_hidden[at, :], w_in[...], NT)
        row_grad[pl.ds(j * 32, 32)] = down.reshape(32, CAP, width).astype(BF16)
        send(j, False)

    @pl.loop(0, hid, step=256)
    def _(n):
        at = pl.ds(pl.multiple_of(n, 256), 256)
        grad_second_ref[at, :] = dot(hidden[:, at], arrived[...].reshape(rows, width), TN)

    @pl.loop(0, hid, step=256)
    def _(n):
        at = pl.ds(pl.multiple_of(n, 256), 256)
        grad_first_ref[:, at] = dot(inputs_t[...], grad_hidden[:, at])

    pltpu.make_async_copy(row_grad.at[0], back_ref.at[me], own_sem).wait()
    most = sent.at[pl.ds(0, 127)]
    pltpu.make_async_copy(most, most, send_sem.at[0]).wait()
    most = row_grad.at[pl.ds(0, 127)]
    pltpu.make_async_copy(most, most, send_sem.at[1]).wait()
    most = back_ref.at[pl.ds(0, 127)]
    pltpu.make_async_copy(most, most, recv_sem.at[4]).wait()


def finish_kernel(back_ref, pick_ref, first_ref, second_ref, grad_in_hbm, first_hbm, second_hbm, grad_in, sems):
    copies = []
    for ref, to, base in ((first_ref, first_hbm, 0), (second_ref, second_hbm, PIECES)):
        step = ref.shape[0] // PIECES
        for p in range(PIECES):
            at = pl.ds(p * step, step)
            copies.append(pltpu.make_async_copy(ref.at[at], to.at[at], sems.at[base + p]))
            copies[-1].start()
    rows, tokens = pick_ref.shape
    grad_in[...] = dot(pick_ref[...], back_ref[...].reshape(rows, grad_in.shape[1]), TN).astype(BF16)
    copies.append(pltpu.make_async_copy(grad_in, grad_in_hbm, sems.at[2 * PIECES]))
    copies[-1].start()
    for c in copies:
        c.wait()


def local(grad_out, gate_prob, expert_index, slot, saved_inputs, w_in, w_out):
    tokens, width = grad_out.shape
    rows, hid = saved_inputs.shape[1], w_in.shape[2]
    experts = rows // CAP
    vmem, hbm = pl.BlockSpec(memory_space=pltpu.VMEM), pl.BlockSpec(memory_space=pl.ANY)
    back, pick, first, second = pl.pallas_call(
        exchange_kernel,
        out_shape=(
            pltpu.VMEM((experts, CAP, width), BF16),
            pltpu.VMEM((rows, tokens), BF16),
            pltpu.VMEM((width, hid), F32),
            pltpu.VMEM((hid, width), F32),
        ),
        in_specs=[hbm] * 7,
        out_specs=(vmem,) * 4,
        scratch_shapes=[
            pltpu.VMEM((1, tokens), F32),
            pltpu.VMEM((1, tokens), jnp.int32),
            pltpu.VMEM((1, tokens), jnp.int32),
            pltpu.VMEM((tokens, width), BF16),
            pltpu.VMEM((rows, width), BF16),
            pltpu.VMEM((width, rows), BF16),
            pltpu.VMEM((width, hid), BF16),
            pltpu.VMEM((hid, width), BF16),
            pltpu.VMEM((experts, CAP, width), BF16),
            pltpu.VMEM((experts, CAP, width), BF16),
            pltpu.VMEM((experts, CAP, width), BF16),
            pltpu.VMEM((rows, hid), BF16),
            pltpu.VMEM((rows, hid), BF16),
            pltpu.SemaphoreType.DMA((14,)),
            pltpu.SemaphoreType.DMA,
            pltpu.SemaphoreType.DMA((2,)),
            pltpu.SemaphoreType.DMA((5,)),
            pltpu.SemaphoreType.REGULAR,
            pltpu.SemaphoreType.REGULAR,
        ],
        name="exchange",
        compiler_params=pltpu.CompilerParams(collective_id=0, has_side_effects=True, vmem_limit_bytes=40 << 20),
    )(
        gate_prob.reshape(1, tokens),
        expert_index.reshape(1, tokens),
        slot.reshape(1, tokens),
        grad_out,
        saved_inputs[0],
        w_in[0],
        w_out[0],
    )
    grad_in, grad_first, grad_second = pl.pallas_call(
        finish_kernel,
        out_shape=(
            jax.ShapeDtypeStruct((tokens, width), BF16),
            jax.ShapeDtypeStruct((width, hid), F32),
            jax.ShapeDtypeStruct((hid, width), F32),
        ),
        in_specs=[vmem] * 4,
        out_specs=(hbm,) * 3,
        scratch_shapes=[pltpu.VMEM((tokens, width), BF16), pltpu.SemaphoreType.DMA((2 * PIECES + 1,))],
        name="finish",
        compiler_params=pltpu.CompilerParams(vmem_limit_bytes=24 << 20),
    )(*(pltpu.with_memory_space_constraint(a, pltpu.VMEM) for a in (back, pick, first, second)))
    return grad_in, grad_first[None], grad_second[None]


def solution(mesh):
    spec1, spec2, spec3 = (P(("group", "rank"), *(None,) * n) for n in range(3))
    return jax.shard_map(
        local,
        mesh=mesh,
        in_specs=(spec2, spec1, spec1, spec1, spec3, spec3, spec3),
        out_specs=(spec2, spec3, spec3),
        check_vma=False,
    )
```

```python
import functools

import jax
import jax.numpy as jnp
from jax import lax
from jax.experimental import pallas as pl
from jax.experimental.pallas import tpu as pltpu
from jax.sharding import PartitionSpec as P

MESH = pl.DeviceIdType.MESH
BF16, F32 = jnp.bfloat16, jnp.float32
NT = (((1,), (1,)), ((), ()))
TN = (((0,), (0,)), ((), ()))
GROUPS = (((1, 1), (3, 1)), ((2, 1), (0, 0)), ((1, 0), (3, 0)), ((2, 0), (0, 1)))
CAP = 8
SIDE = 4
PIECES = 1


def dot(a, b, dims=(((1,), (0,)), ((), ()))):
    return lax.dot_general(a, b, dims, preferred_element_type=F32)


def exchange_kernel(
    gate_hbm, expert_hbm, slot_hbm, grad_hbm, inputs_hbm, w_in_hbm, w_out_hbm,
    back_ref, pick_ref, grad_first_ref, grad_second_ref,
    gate_ref, expert_ref, slot_ref, grad, inputs, inputs_t, w_in, w_out, sent, arrived, row_grad, hidden, grad_hidden,
    load_sem, own_sem, send_sem, recv_sem, sync_a, sync_b,
):
    group, rank = lax.axis_index("group"), lax.axis_index("rank")
    x, y, z, core = rank // SIDE, rank % SIDE, group // 2, group % 2
    me = group * 16 + rank
    tokens, width = grad.shape
    rows = inputs.shape[0]
    hid = hidden.shape[1]
    quarter = rows // 4

    def device(dx, dy, dz, dc):
        return (lax.rem(z + dz, SIDE) * 2 + lax.rem(core + dc, 2), lax.rem(x + dx, SIDE) * SIDE + lax.rem(y + dy, SIDE))

    barrier = pltpu.get_barrier_semaphore()
    others = [device(i, k, l, c) for l in (1, 3, 2, 0) for k in range(4) for i in range(4) for c in range(2) if i + k + l + c > 0]
    for d in others:
        pl.semaphore_signal(barrier, inc=1, device_id=d, device_id_type=MESH)

    load_tokens = [
        pltpu.make_async_copy(src, dst, load_sem.at[11 + i])
        for i, (src, dst) in enumerate(((gate_hbm, gate_ref), (expert_hbm, expert_ref), (slot_hbm, slot_ref)))
    ]
    for c in load_tokens:
        c.start()
    load_grad = pltpu.make_async_copy(grad_hbm, grad, load_sem.at[0])
    load_grad.start()
    load_w_in = pltpu.make_async_copy(w_in_hbm, w_in, load_sem.at[1])
    load_w_in.start()
    load_rows = []
    for j, pair in enumerate(GROUPS):
        for i, (dz, dc) in enumerate(pair):
            g = lax.rem(z + dz, SIDE) * 2 + lax.rem(core + dc, 2)
            at = (j * 2 + i) * 128
            load_rows.append(
                pltpu.make_async_copy(
                    inputs_hbm.at[pl.ds(pl.multiple_of(g * 128, 128), 128)], inputs.at[pl.ds(at, 128)], load_sem.at[2 + j * 2 + i]
                )
            )
            load_rows[-1].start()
    load_w_out = pltpu.make_async_copy(w_out_hbm, w_out, load_sem.at[10])
    load_w_out.start()

    for c in load_tokens:
        c.wait()
    gate = gate_ref[...]
    high = gate.astype(BF16)
    rest = gate - high.astype(F32)
    middle = rest.astype(BF16)
    low = (rest - middle.astype(F32)).astype(BF16)
    gates = [jnp.broadcast_to(part, (128, tokens)) for part in (high, middle, low)]
    target = jnp.where(slot_ref[...] >= 0, expert_ref[...] * CAP + slot_ref[...], -1)
    load_grad.wait()

    def group_at(j, i):
        dz, dc = GROUPS[j][i]
        return lax.rem(z + dz, SIDE) * 2 + lax.rem(core + dc, 2)

    def fill(g):
        at = lax.broadcasted_iota(jnp.int32, (128, tokens), 0) + g * 128
        table = (at == target).astype(BF16)
        pick_ref[pl.ds(pl.multiple_of(g * 128, 128), 128), :] = table
        factor = dot(table, gates[0], NT) + dot(table, gates[1], NT) + dot(table, gates[2], NT)
        factor = jnp.concatenate([factor] * (width // 128), axis=1)
        block = dot(table, grad[...]) * factor
        sent[pl.ds(g * 16, 16)] = block.reshape(16, CAP, width).astype(BF16)

    def send(j, out):
        def copy_of(i, dx, dy):
            g = group_at(j, i)
            there = i if GROUPS[j][i][0] in (0, 2) else 1 - i
            r = lax.rem(x + dx, SIDE) * SIDE + lax.rem(y + dy, SIDE)
            if out:
                src, dst, end = sent.at[g * 16 + r], arrived.at[(j * 2 + there) * 16 + rank], (send_sem.at[0], recv_sem.at[j])
            else:
                src, dst, end = row_grad.at[(j * 2 + i) * 16 + r], back_ref.at[me], (send_sem.at[1], recv_sem.at[4])
            return src, dst, end, (g, r)

        def start(i, dx, dy):
            src, dst, end, d = copy_of(i, dx, dy)
            pltpu.make_async_remote_copy(src, dst, *end, device_id=d, device_id_type=MESH).start()

        def swing(q):
            return q + q // 2 - 2 * (q // 3)

        def one(k, carry):
            for i in range(2):
                start(i, swing(k % 4), swing((k + k // 4) % 4))
            return carry

        own = (0, 0) in GROUPS[j]
        if own:
            start(0, 0, 0)
            src, dst, _, _ = copy_of(1, 0, 0)
            pltpu.make_async_copy(src, dst, own_sem).start()
        lax.fori_loop(1 if own else 0, 16, one, 0)

    for j in range(4):
        fill(group_at(j, 0))
        fill(group_at(j, 1))
        if j == 0:
            pl.semaphore_wait(barrier, 127)
        send(j, True)

    load_w_in.wait()
    for c in load_rows:
        c.wait()

    @pl.loop(0, 4)
    def _(p):
        at = pl.ds(pl.multiple_of(p * quarter, quarter), quarter)
        for n in range(0, hid, 512):
            pre = dot(inputs[at, :], w_in[:, n : n + 512])
            hidden[at, n : n + 512] = jnp.maximum(pre, 0.0).astype(BF16)

    inputs_t[...] = inputs[...].T
    load_w_out.wait()

    for j in range(4):
        count = 31 if (0, 0) in GROUPS[j] else 32
        got = arrived.at[pl.ds(0, count)]
        pltpu.make_async_copy(got, got, recv_sem.at[j]).wait()
        if count == 31:
            pltpu.make_async_copy(sent.at[me], arrived.at[j * 32 + rank], own_sem).wait()
        block = arrived[pl.ds(j * 32, 32)].reshape(quarter, width)
        at = pl.ds(j * quarter, quarter)
        for n in range(0, hid, 512):
            up = dot(block, w_out[n : n + 512, :], NT)
            grad_hidden[at, n : n + 512] = jnp.where(hidden[at, n : n + 512].astype(F32) > 0, up, 0.0).astype(BF16)
        down = dot(grad_hidden[at, :], w_in[...], NT)
        row_grad[pl.ds(j * 32, 32)] = down.reshape(32, CAP, width).astype(BF16)
        send(j, False)

    @pl.loop(0, hid, step=256)
    def _(n):
        at = pl.ds(pl.multiple_of(n, 256), 256)
        grad_second_ref[at, :] = dot(hidden[:, at], arrived[...].reshape(rows, width), TN)

    @pl.loop(0, hid, step=256)
    def _(n):
        at = pl.ds(pl.multiple_of(n, 256), 256)
        grad_first_ref[:, at] = dot(inputs_t[...], grad_hidden[:, at])

    pltpu.make_async_copy(row_grad.at[0], back_ref.at[me], own_sem).wait()
    most = sent.at[pl.ds(0, 127)]
    pltpu.make_async_copy(most, most, send_sem.at[0]).wait()
    most = row_grad.at[pl.ds(0, 127)]
    pltpu.make_async_copy(most, most, send_sem.at[1]).wait()
    most = back_ref.at[pl.ds(0, 127)]
    pltpu.make_async_copy(most, most, recv_sem.at[4]).wait()


def finish_kernel(back_ref, pick_ref, first_ref, second_ref, grad_in_hbm, first_hbm, second_hbm, grad_in, sems):
    copies = []
    for ref, to, base in ((first_ref, first_hbm, 0), (second_ref, second_hbm, PIECES)):
        step = ref.shape[0] // PIECES
        for p in range(PIECES):
            at = pl.ds(p * step, step)
            copies.append(pltpu.make_async_copy(ref.at[at], to.at[at], sems.at[base + p]))
            copies[-1].start()
    rows, tokens = pick_ref.shape
    grad_in[...] = dot(pick_ref[...], back_ref[...].reshape(rows, grad_in.shape[1]), TN).astype(BF16)
    copies.append(pltpu.make_async_copy(grad_in, grad_in_hbm, sems.at[2 * PIECES]))
    copies[-1].start()
    for c in copies:
        c.wait()


def local(grad_out, gate_prob, expert_index, slot, saved_inputs, w_in, w_out):
    tokens, width = grad_out.shape
    rows, hid = saved_inputs.shape[1], w_in.shape[2]
    experts = rows // CAP
    vmem, hbm = pl.BlockSpec(memory_space=pltpu.VMEM), pl.BlockSpec(memory_space=pl.ANY)
    back, pick, first, second = pl.pallas_call(
        exchange_kernel,
        out_shape=(
            pltpu.VMEM((experts, CAP, width), BF16),
            pltpu.VMEM((rows, tokens), BF16),
            pltpu.VMEM((width, hid), F32),
            pltpu.VMEM((hid, width), F32),
        ),
        in_specs=[hbm] * 7,
        out_specs=(vmem,) * 4,
        scratch_shapes=[
            pltpu.VMEM((1, tokens), F32),
            pltpu.VMEM((1, tokens), jnp.int32),
            pltpu.VMEM((1, tokens), jnp.int32),
            pltpu.VMEM((tokens, width), BF16),
            pltpu.VMEM((rows, width), BF16),
            pltpu.VMEM((width, rows), BF16),
            pltpu.VMEM((width, hid), BF16),
            pltpu.VMEM((hid, width), BF16),
            pltpu.VMEM((experts, CAP, width), BF16),
            pltpu.VMEM((experts, CAP, width), BF16),
            pltpu.VMEM((experts, CAP, width), BF16),
            pltpu.VMEM((rows, hid), BF16),
            pltpu.VMEM((rows, hid), BF16),
            pltpu.SemaphoreType.DMA((14,)),
            pltpu.SemaphoreType.DMA,
            pltpu.SemaphoreType.DMA((2,)),
            pltpu.SemaphoreType.DMA((5,)),
            pltpu.SemaphoreType.REGULAR,
            pltpu.SemaphoreType.REGULAR,
        ],
        name="exchange",
        compiler_params=pltpu.CompilerParams(collective_id=0, has_side_effects=True, vmem_limit_bytes=40 << 20),
    )(
        gate_prob.reshape(1, tokens),
        expert_index.reshape(1, tokens),
        slot.reshape(1, tokens),
        grad_out,
        saved_inputs[0],
        w_in[0],
        w_out[0],
    )
    grad_in, grad_first, grad_second = pl.pallas_call(
        finish_kernel,
        out_shape=(
            jax.ShapeDtypeStruct((tokens, width), BF16),
            jax.ShapeDtypeStruct((width, hid), F32),
            jax.ShapeDtypeStruct((hid, width), F32),
        ),
        in_specs=[vmem] * 4,
        out_specs=(hbm,) * 3,
        scratch_shapes=[pltpu.VMEM((tokens, width), BF16), pltpu.SemaphoreType.DMA((2 * PIECES + 1,))],
        name="finish",
        compiler_params=pltpu.CompilerParams(vmem_limit_bytes=24 << 20),
    )(*(pltpu.with_memory_space_constraint(a, pltpu.VMEM) for a in (back, pick, first, second)))
    return grad_in, grad_first[None], grad_second[None]


def solution(mesh):
    spec1, spec2, spec3 = (P(("group", "rank"), *(None,) * n) for n in range(3))
    return jax.shard_map(
        local,
        mesh=mesh,
        in_specs=(spec2, spec1, spec1, spec1, spec3, spec3, spec3),
        out_specs=(spec2, spec3, spec3),
        check_vma=False,
    )
```

```python
import functools

import jax
import jax.numpy as jnp
from jax import lax
from jax.experimental import pallas as pl
from jax.experimental.pallas import tpu as pltpu
from jax.sharding import PartitionSpec as P

MESH = pl.DeviceIdType.MESH
BF16, F32 = jnp.bfloat16, jnp.float32
NT = (((1,), (1,)), ((), ()))
TN = (((0,), (0,)), ((), ()))
GROUPS = (((1, 1), (3, 1)), ((2, 1), (0, 0)), ((1, 0), (3, 0)), ((2, 0), (0, 1)))
CAP = 8
SIDE = 4
PIECES = 1


def dot(a, b, dims=(((1,), (0,)), ((), ()))):
    return lax.dot_general(a, b, dims, preferred_element_type=F32)


def exchange_kernel(
    gate_hbm, expert_hbm, slot_hbm, grad_hbm, inputs_hbm, w_in_hbm, w_out_hbm,
    back_ref, pick_ref, grad_first_ref, grad_second_ref,
    gate_ref, expert_ref, slot_ref, grad, inputs, inputs_t, w_in, w_out, sent, arrived, row_grad, hidden, grad_hidden,
    load_sem, own_sem, send_sem, recv_sem, sync_a, sync_b,
):
    group, rank = lax.axis_index("group"), lax.axis_index("rank")
    x, y, z, core = rank // SIDE, rank % SIDE, group // 2, group % 2
    me = group * 16 + rank
    tokens, width = grad.shape
    rows = inputs.shape[0]
    hid = hidden.shape[1]
    quarter = rows // 4

    def device(dx, dy, dz, dc):
        return (lax.rem(z + dz, SIDE) * 2 + lax.rem(core + dc, 2), lax.rem(x + dx, SIDE) * SIDE + lax.rem(y + dy, SIDE))

    barrier = pltpu.get_barrier_semaphore()
    others = [device(i, k, l, c) for l in (1, 3, 2, 0) for k in range(4) for i in range(4) for c in range(2) if i + k + l + c > 0]
    for d in others:
        pl.semaphore_signal(barrier, inc=1, device_id=d, device_id_type=MESH)

    load_tokens = [
        pltpu.make_async_copy(src, dst, load_sem.at[11 + i])
        for i, (src, dst) in enumerate(((gate_hbm, gate_ref), (expert_hbm, expert_ref), (slot_hbm, slot_ref)))
    ]
    for c in load_tokens:
        c.start()
    load_grad = pltpu.make_async_copy(grad_hbm, grad, load_sem.at[0])
    load_grad.start()
    load_w_in = pltpu.make_async_copy(w_in_hbm, w_in, load_sem.at[1])
    load_w_in.start()
    load_rows = []
    for j, pair in enumerate(GROUPS):
        for i, (dz, dc) in enumerate(pair):
            g = lax.rem(z + dz, SIDE) * 2 + lax.rem(core + dc, 2)
            at = (j * 2 + i) * 128
            load_rows.append(
                pltpu.make_async_copy(
                    inputs_hbm.at[pl.ds(pl.multiple_of(g * 128, 128), 128)], inputs.at[pl.ds(at, 128)], load_sem.at[2 + j * 2 + i]
                )
            )
            load_rows[-1].start()
    load_w_out = pltpu.make_async_copy(w_out_hbm, w_out, load_sem.at[10])
    load_w_out.start()

    for c in load_tokens:
        c.wait()
    gate = gate_ref[...]
    high = gate.astype(BF16)
    rest = gate - high.astype(F32)
    middle = rest.astype(BF16)
    low = (rest - middle.astype(F32)).astype(BF16)
    gates = [jnp.broadcast_to(part, (128, tokens)) for part in (high, middle, low)]
    target = jnp.where(slot_ref[...] >= 0, expert_ref[...] * CAP + slot_ref[...], -1)
    load_grad.wait()

    def group_at(j, i):
        dz, dc = GROUPS[j][i]
        return lax.rem(z + dz, SIDE) * 2 + lax.rem(core + dc, 2)

    def fill(g):
        at = lax.broadcasted_iota(jnp.int32, (128, tokens), 0) + g * 128
        table = (at == target).astype(BF16)
        pick_ref[pl.ds(pl.multiple_of(g * 128, 128), 128), :] = table
        factor = dot(table, gates[0], NT) + dot(table, gates[1], NT) + dot(table, gates[2], NT)
        factor = jnp.concatenate([factor] * (width // 128), axis=1)
        block = dot(table, grad[...]) * factor
        sent[pl.ds(g * 16, 16)] = block.reshape(16, CAP, width).astype(BF16)

    def send(j, out):
        def copy_of(i, dx, dy):
            g = group_at(j, i)
            there = i if GROUPS[j][i][0] in (0, 2) else 1 - i
            r = lax.rem(x + dx, SIDE) * SIDE + lax.rem(y + dy, SIDE)
            if out:
                src, dst, end = sent.at[g * 16 + r], arrived.at[(j * 2 + there) * 16 + rank], (send_sem.at[0], recv_sem.at[j])
            else:
                src, dst, end = row_grad.at[(j * 2 + i) * 16 + r], back_ref.at[me], (send_sem.at[1], recv_sem.at[4])
            return src, dst, end, (g, r)

        def start(i, dx, dy):
            src, dst, end, d = copy_of(i, dx, dy)
            pltpu.make_async_remote_copy(src, dst, *end, device_id=d, device_id_type=MESH).start()

        def swing(q):
            return q + q // 2 - 2 * (q // 3)

        def one(k, carry):
            for i in range(2):
                start(i, swing((k + k // 4) % 4), swing(k % 4))
            return carry

        own = (0, 0) in GROUPS[j]
        if own:
            start(0, 0, 0)
            src, dst, _, _ = copy_of(1, 0, 0)
            pltpu.make_async_copy(src, dst, own_sem).start()
        lax.fori_loop(1 if own else 0, 16, one, 0)

    for j in range(4):
        fill(group_at(j, 0))
        fill(group_at(j, 1))
        if j == 0:
            pl.semaphore_wait(barrier, 127)
        send(j, True)

    load_w_in.wait()
    for c in load_rows:
        c.wait()

    @pl.loop(0, 4)
    def _(p):
        at = pl.ds(pl.multiple_of(p * quarter, quarter), quarter)
        for n in range(0, hid, 512):
            pre = dot(inputs[at, :], w_in[:, n : n + 512])
            hidden[at, n : n + 512] = jnp.maximum(pre, 0.0).astype(BF16)
            grad_hidden[at, n : n + 512] = (pre > 0).astype(BF16)

    inputs_t[...] = inputs[...].T
    load_w_out.wait()

    for j in range(4):
        count = 31 if (0, 0) in GROUPS[j] else 32
        got = arrived.at[pl.ds(0, count)]
        pltpu.make_async_copy(got, got, recv_sem.at[j]).wait()
        if count == 31:
            pltpu.make_async_copy(sent.at[me], arrived.at[j * 32 + rank], own_sem).wait()
        block = arrived[pl.ds(j * 32, 32)].reshape(quarter, width)
        at = pl.ds(j * quarter, quarter)
        for n in range(0, hid, 512):
            up = dot(block, w_out[n : n + 512, :], NT)
            grad_hidden[at, n : n + 512] = jnp.where(grad_hidden[at, n : n + 512].astype(F32) > 0, up, 0.0).astype(BF16)
        down = dot(grad_hidden[at, :], w_in[...], NT)
        row_grad[pl.ds(j * 32, 32)] = down.reshape(32, CAP, width).astype(BF16)
        send(j, False)

    @pl.loop(0, hid, step=256)
    def _(n):
        at = pl.ds(pl.multiple_of(n, 256), 256)
        grad_second_ref[at, :] = dot(hidden[:, at], arrived[...].reshape(rows, width), TN)

    @pl.loop(0, hid, step=256)
    def _(n):
        at = pl.ds(pl.multiple_of(n, 256), 256)
        grad_first_ref[:, at] = dot(inputs_t[...], grad_hidden[:, at])

    pltpu.make_async_copy(row_grad.at[0], back_ref.at[me], own_sem).wait()
    most = sent.at[pl.ds(0, 127)]
    pltpu.make_async_copy(most, most, send_sem.at[0]).wait()
    most = row_grad.at[pl.ds(0, 127)]
    pltpu.make_async_copy(most, most, send_sem.at[1]).wait()
    most = back_ref.at[pl.ds(0, 127)]
    pltpu.make_async_copy(most, most, recv_sem.at[4]).wait()


def finish_kernel(back_ref, pick_ref, first_ref, second_ref, grad_in_hbm, first_hbm, second_hbm, grad_in, sems):
    copies = []
    for ref, to, base in ((first_ref, first_hbm, 0), (second_ref, second_hbm, PIECES)):
        step = ref.shape[0] // PIECES
        for p in range(PIECES):
            at = pl.ds(p * step, step)
            copies.append(pltpu.make_async_copy(ref.at[at], to.at[at], sems.at[base + p]))
            copies[-1].start()
    rows, tokens = pick_ref.shape
    grad_in[...] = dot(pick_ref[...], back_ref[...].reshape(rows, grad_in.shape[1]), TN).astype(BF16)
    copies.append(pltpu.make_async_copy(grad_in, grad_in_hbm, sems.at[2 * PIECES]))
    copies[-1].start()
    for c in copies:
        c.wait()


def local(grad_out, gate_prob, expert_index, slot, saved_inputs, w_in, w_out):
    tokens, width = grad_out.shape
    rows, hid = saved_inputs.shape[1], w_in.shape[2]
    experts = rows // CAP
    vmem, hbm = pl.BlockSpec(memory_space=pltpu.VMEM), pl.BlockSpec(memory_space=pl.ANY)
    back, pick, first, second = pl.pallas_call(
        exchange_kernel,
        out_shape=(
            pltpu.VMEM((experts, CAP, width), BF16),
            pltpu.VMEM((rows, tokens), BF16),
            pltpu.VMEM((width, hid), F32),
            pltpu.VMEM((hid, width), F32),
        ),
        in_specs=[hbm] * 7,
        out_specs=(vmem,) * 4,
        scratch_shapes=[
            pltpu.VMEM((1, tokens), F32),
            pltpu.VMEM((1, tokens), jnp.int32),
            pltpu.VMEM((1, tokens), jnp.int32),
            pltpu.VMEM((tokens, width), BF16),
            pltpu.VMEM((rows, width), BF16),
            pltpu.VMEM((width, rows), BF16),
            pltpu.VMEM((width, hid), BF16),
            pltpu.VMEM((hid, width), BF16),
            pltpu.VMEM((experts, CAP, width), BF16),
            pltpu.VMEM((experts, CAP, width), BF16),
            pltpu.VMEM((experts, CAP, width), BF16),
            pltpu.VMEM((rows, hid), BF16),
            pltpu.VMEM((rows, hid), BF16),
            pltpu.SemaphoreType.DMA((14,)),
            pltpu.SemaphoreType.DMA,
            pltpu.SemaphoreType.DMA((2,)),
            pltpu.SemaphoreType.DMA((5,)),
            pltpu.SemaphoreType.REGULAR,
            pltpu.SemaphoreType.REGULAR,
        ],
        name="exchange",
        compiler_params=pltpu.CompilerParams(collective_id=0, has_side_effects=True, vmem_limit_bytes=40 << 20),
    )(
        gate_prob.reshape(1, tokens),
        expert_index.reshape(1, tokens),
        slot.reshape(1, tokens),
        grad_out,
        saved_inputs[0],
        w_in[0],
        w_out[0],
    )
    grad_in, grad_first, grad_second = pl.pallas_call(
        finish_kernel,
        out_shape=(
            jax.ShapeDtypeStruct((tokens, width), BF16),
            jax.ShapeDtypeStruct((width, hid), F32),
            jax.ShapeDtypeStruct((hid, width), F32),
        ),
        in_specs=[vmem] * 4,
        out_specs=(hbm,) * 3,
        scratch_shapes=[pltpu.VMEM((tokens, width), BF16), pltpu.SemaphoreType.DMA((2 * PIECES + 1,))],
        name="finish",
        compiler_params=pltpu.CompilerParams(vmem_limit_bytes=24 << 20),
    )(*(pltpu.with_memory_space_constraint(a, pltpu.VMEM) for a in (back, pick, first, second)))
    return grad_in, grad_first[None], grad_second[None]


def solution(mesh):
    spec1, spec2, spec3 = (P(("group", "rank"), *(None,) * n) for n in range(3))
    return jax.shard_map(
        local,
        mesh=mesh,
        in_specs=(spec2, spec1, spec1, spec1, spec3, spec3, spec3),
        out_specs=(spec2, spec3, spec3),
        check_vma=False,
    )
```
